32 devices in a mesh: groups: 2 (over y), doc: 16 (over z, x, core).
Axes of the slice: x: 2, y: 2, z: 4, core: 2. Of those that a mesh axis runs over, the one named last changes fastest.
Arguments:
- queries: bfloat16 [32, 32, 128], P(('groups', 'doc')), parts along dimension 0, may hold values from -0.015625 to 0.015625
- doc_tokens: bfloat16 [4096, 128, 128], P(('groups', 'doc')), parts along dimension 0, may hold values from -6 to 6
- doc_lengths: int32 [4096], P(('groups', 'doc')), parts along dimension 0, may hold values from 1 to 128, as said below
- candidates: int32 [32, 256], P(('groups', 'doc')), parts along dimension 0, may hold values from 0 to 2047, as said below
Outputs:
- scores: float32 [32, 256], P(('groups', 'doc')), parts along dimension 0
The draws below stay inside these ranges and needn't reach their ends.
There are 2 independent parts, one for each index of `groups`. The reference program is written for one: setup_inputs(seed, part) draws one part's arguments, and reference() takes and returns one part's arrays. A program takes and returns all parts, laid end to end along the dimension named above; each array names one. Nothing has to cross between parts.
Inputs may be any that keep to these rules, and one draw needn't show every extreme that they name: Passage ids. Device d holds passages d * 128 to (d + 1) * 128 - 1 and queries d * 1 to (d + 1) - 1. At most 48 candidates of one query lie on any one device; in every draw one device holds exactly 48 candidates of every query. A query may name a passage more than once. `doc_lengths`: the first passage of every device has all 128 tokens.
All inputs are finite; a program needn't handle non-finite values.
Results may differ from the reference program's by a relative error of at most 0.0003.
Values may be sent and summed in bfloat16 or wider, within the bound.
A program may use at most 64 MiB of HBM per device.

```python
import jax
import jax.numpy as jnp
from jax import lax

DIM = 128
QT = 32
DT = 128
CAND = 256
QDEV = 1
DOC_DEV = 128
KMAX = 48
QUERIES = 16
DOCS = 2048
N_DOC = 16


def draw_doc_lengths(key, part):
    key = jax.random.fold_in(key, 7)
    values = jax.random.randint(key, (DOC_DEV * N_DOC,), 1, DT + 1).astype(jnp.int32)
    places = jnp.arange(DOC_DEV * N_DOC).astype(jnp.int32)
    return jnp.where(places % DOC_DEV == 0, DT, values).astype(jnp.int32)


def draw_candidates(key, part):
    key = jax.random.fold_in(key, 11)
    first, second, third, fourth = jax.random.split(key, 4)
    pool = N_DOC * KMAX
    count = N_DOC * QDEV
    hottest = jax.random.randint(first, (), 0, N_DOC).astype(jnp.int32)
    entries = jnp.arange(pool).astype(jnp.int32)
    owner_of = entries // KMAX
    noise = jax.random.randint(second, (count, pool), 0, 1024).astype(jnp.int32)
    ranking = noise * pool + entries[None, :] + (owner_of == hottest).astype(jnp.int32)[None, :] * (1024 * pool)
    order = jnp.argsort(-ranking, axis=1, stable=True)[:, :CAND].astype(jnp.int32)
    owners = order // KMAX
    shuffle_keys = jax.random.randint(third, (count, CAND), 0, 1024).astype(jnp.int32) * CAND + jnp.arange(CAND).astype(jnp.int32)[None, :]
    mixing = jnp.argsort(shuffle_keys, axis=1, stable=True).astype(jnp.int32)
    owners = jnp.take_along_axis(owners, mixing, axis=1)
    within = jax.random.randint(fourth, (count, CAND), 0, DOC_DEV).astype(jnp.int32)
    return (owners * DOC_DEV + within).astype(jnp.int32)


def shard_levels(key, shape, shards, low, high):
    level = 1.0
    for dim, blocks in shards:
        draws = jax.random.uniform(jax.random.fold_in(jax.random.fold_in(key, 6), dim), (blocks,), jnp.float32, low / len(shards), high / len(shards))
        level = level * jnp.repeat(jnp.exp(draws), shape[dim] // blocks).reshape((-1,) + (1,) * (len(shape) - 1 - dim))
    return level


def centred(own_key, extent, scale, bound, cuts=(), kind=jnp.bfloat16):
    values = scale * jax.random.normal(own_key, extent, jnp.float32)
    if cuts:
        values = values * shard_levels(own_key, extent, cuts, -0.22, 0.18)
    return jnp.clip(values, -bound, bound).astype(kind)


def setup_inputs(seed: int = 0, part: int = 0) -> dict:
    seeds = jax.random.split(jax.random.key(seed), 5)
    part_keys = jax.random.split(jax.random.fold_in(seeds[4], part), 5)
    return {
        "queries": centred(part_keys[0], (QUERIES, QT, DIM), (QT * QT * DIM) ** -0.5, 0.015625, ((0, 16),)),
        "doc_tokens": centred(part_keys[1], (DOCS, DT, DIM), 1.0, 6.0, ((0, 16),)),
        "doc_lengths": draw_doc_lengths(jax.random.fold_in(jax.random.fold_in(seeds[4], part), 71), part),
        "candidates": draw_candidates(jax.random.fold_in(jax.random.fold_in(seeds[4], part), 71), part),
    }


def reference(queries, doc_tokens, doc_lengths, candidates):
    positions = jnp.arange(DT).astype(jnp.int32)

    def one_query(packed):
        query, picks = packed
        docs = doc_tokens[picks].astype(jnp.float32)
        lengths = doc_lengths[picks]
        similar = jnp.einsum("ak,ctk->cat", query.astype(jnp.float32), docs, precision=lax.Precision.HIGHEST)
        keep = positions[None, None, :] < lengths[:, None, None]
        best = jnp.max(jnp.where(keep, similar, -jnp.inf), axis=2)
        return jnp.sum(best, axis=1)

    return lax.map(one_query, (queries, candidates))
```

```python
import functools

import jax
import jax.numpy as jnp
from jax import lax
from jax.experimental import pallas as pl
from jax.experimental.pallas import tpu as pltpu
from jax.sharding import PartitionSpec as P

LANES = 256
CHUNKS = 8
UNROLL = 8


def split3(x):
    hi = x.astype(jnp.bfloat16)
    rest = x - hi.astype(jnp.float32)
    mid = rest.astype(jnp.bfloat16)
    lo = (rest - mid.astype(jnp.float32)).astype(jnp.bfloat16)
    return hi, mid, lo


def nt_dot(a, b):
    return lax.dot_general(a, b, (((1,), (1,)), ((), ())), preferred_element_type=jnp.float32)


def kernel(
    n,
    q_hbm,
    docs_hbm,
    lengths_hbm,
    cand_hbm,
    out_ref,
    docs,
    lengths,
    cand,
    queries,
    best,
    scores,
    table,
    doc_sem,
    small_sem,
    q_send,
    q_recv,
    s_send,
    s_recv,
):
    me = lax.axis_index("doc")
    count, doc_len, feature = docs.shape
    query_len = queries.shape[1]
    width = min(n, LANES // query_len)
    groups = n // width
    chunk = count // CHUNKS

    own = pltpu.make_async_copy(q_hbm.at[0], queries.at[me], small_sem.at[0])
    own.start()
    len_copy = pltpu.make_async_copy(lengths_hbm, lengths, small_sem.at[1])
    len_copy.start()
    doc_copies = []
    for c in range(CHUNKS):
        rows = pl.ds(c * chunk, chunk)
        copy = pltpu.make_async_copy(docs_hbm.at[rows], docs.at[rows], doc_sem.at[c])
        copy.start()
        doc_copies.append(copy)
    cand_copy = pltpu.make_async_copy(cand_hbm, cand, small_sem.at[2])
    cand_copy.start()

    barrier = pltpu.get_barrier_semaphore()

    @pl.loop(1, n)
    def _(p):
        pl.semaphore_signal(
            barrier,
            inc=1,
            device_id={"doc": lax.rem(me + p, n)},
            device_id_type=pl.DeviceIdType.MESH,
        )

    own.wait()
    pl.semaphore_wait(barrier, n - 1)

    def query_copy(peer, slot):
        return pltpu.make_async_remote_copy(
            src_ref=queries.at[me],
            dst_ref=queries.at[slot],
            send_sem=q_send.at[peer],
            recv_sem=q_recv.at[slot],
            device_id={"doc": peer},
            device_id_type=pl.DeviceIdType.MESH,
        )

    def score_copy(peer, slot):
        return pltpu.make_async_remote_copy(
            src_ref=scores.at[peer],
            dst_ref=table.at[slot],
            send_sem=s_send.at[peer],
            recv_sem=s_recv.at[slot],
            device_id={"doc": peer},
            device_id_type=pl.DeviceIdType.MESH,
        )

    home = me // width
    place = lax.rem(me, width)

    def peer_at(g, j):
        return lax.rem(home + g, groups) * width + lax.rem(place + j, width)

    @pl.loop(1, n)
    def _(p):
        query_copy(peer_at(p // width, lax.rem(p, width)), me).start()

    len_copy.wait()

    rows_of = lax.broadcasted_iota(jnp.int32, (doc_len, feature), 0)
    for c in range(CHUNKS):
        doc_copies[c].wait()

        @pl.loop(c * chunk, (c + 1) * chunk)
        def _(d):
            doc = docs[d]
            docs[d] = jnp.where(rows_of < lengths[0, d], doc, doc[0:1])

    lane_query = lax.broadcasted_iota(jnp.int32, (width, width * query_len), 1) // query_len
    row_query = lax.broadcasted_iota(jnp.int32, (width, width * query_len), 0)
    member = (lane_query == row_query).astype(jnp.bfloat16)

    @pl.loop(0, groups)
    def _(g):
        first = lax.rem(home + g, groups) * width

        @pl.loop(0, width)
        def _(j):
            @pl.when(first + j != me)
            def _():
                query_copy(first + j, first + j).wait_recv()

        q = queries[pl.ds(first, width)].reshape(width * query_len, feature)

        @pl.loop(0, count // UNROLL)
        def _(b):
            start = pl.multiple_of(b * UNROLL, UNROLL)
            parts = []
            for u in range(UNROLL):
                similar = nt_dot(docs[start + u], q)
                parts.append(jnp.max(similar, axis=0, keepdims=True))
            best[pl.ds(start, UNROLL), :] = jnp.concatenate(parts, axis=0)

        hi, mid, lo = split3(best[...])
        total = nt_dot(member, hi) + nt_dot(member, mid) + nt_dot(member, lo)
        for j in range(width):
            scores[first + j] = total[j : j + 1]

        @pl.loop(0, width)
        def _(j):
            peer = first + lax.rem(place + j, width)

            @pl.when(peer != me)
            def _():
                score_copy(peer, me).start()

    table[me] = scores[me]
    cand_copy.wait()

    @pl.loop(1, n)
    def _(p):
        peer = lax.rem(me + p, n)
        score_copy(peer, peer).wait_recv()

    ids = cand[...]
    owner = ids // count
    local = ids - owner * count
    cands = ids.shape[1]
    pick = (lax.broadcasted_iota(jnp.int32, (count, cands), 0) == local).astype(jnp.bfloat16)
    hi, mid, lo = split3(table[...].reshape(n, count))
    found = (
        jnp.dot(hi, pick, preferred_element_type=jnp.float32)
        + jnp.dot(mid, pick, preferred_element_type=jnp.float32)
        + jnp.dot(lo, pick, preferred_element_type=jnp.float32)
    )
    mine = lax.broadcasted_iota(jnp.int32, (n, cands), 0) == owner
    out_ref[...] = jnp.sum(jnp.where(mine, found, 0.0), axis=0, keepdims=True)

    @pl.loop(1, n)
    def _(p):
        peer = lax.rem(me + p, n)
        query_copy(peer, me).wait_send()
        score_copy(peer, me).wait_send()


def body(queries, doc_tokens, doc_lengths, candidates):
    n = lax.axis_size("doc")
    _, query_len, feature = queries.shape
    count, doc_len, _ = doc_tokens.shape
    cands = candidates.shape[1]
    width = min(n, LANES // query_len)
    hbm = pl.BlockSpec(memory_space=pl.ANY)
    return pl.pallas_call(
        functools.partial(kernel, n),
        out_shape=jax.ShapeDtypeStruct((1, cands), jnp.float32),
        in_specs=[hbm] * 4,
        out_specs=pl.BlockSpec(memory_space=pltpu.VMEM),
        scratch_shapes=[
            pltpu.VMEM((count, doc_len, feature), jnp.bfloat16),
            pltpu.SMEM((1, count), jnp.int32),
            pltpu.VMEM((1, cands), jnp.int32),
            pltpu.VMEM((n, query_len, feature), jnp.bfloat16),
            pltpu.VMEM((count, width * query_len), jnp.float32),
            pltpu.VMEM((n, 1, count), jnp.float32),
            pltpu.VMEM((n, 1, count), jnp.float32),
            pltpu.SemaphoreType.DMA((CHUNKS,)),
            pltpu.SemaphoreType.DMA((3,)),
            pltpu.SemaphoreType.DMA((n,)),
            pltpu.SemaphoreType.DMA((n,)),
            pltpu.SemaphoreType.DMA((n,)),
            pltpu.SemaphoreType.DMA((n,)),
        ],
        compiler_params=pltpu.CompilerParams(
            collective_id=0, has_side_effects=True, vmem_limit_bytes=32 * 1024 * 1024
        ),
        cost_estimate=pl.CostEstimate(
            flops=2 * n * query_len * count * doc_len * feature,
            bytes_accessed=2 * count * doc_len * feature,
            transcendentals=0,
        ),
        name="maxsim",
    )(queries, doc_tokens, doc_lengths.reshape(1, count), candidates)


def solution(mesh):
    placed = (
        P(("groups", "doc"), None, None),
        P(("groups", "doc"), None, None),
        P(("groups", "doc")),
        P(("groups", "doc"), None),
    )
    return jax.shard_map(
        body, mesh=mesh, in_specs=placed, out_specs=P(("groups", "doc"), None), check_vma=False
    )
```

```python
import functools

import jax
import jax.numpy as jnp
from jax import lax
from jax.experimental import pallas as pl
from jax.experimental.pallas import tpu as pltpu
from jax.sharding import PartitionSpec as P

LANES = 256
CHUNKS = 8
UNROLL = 64


def split3(x):
    hi = x.astype(jnp.bfloat16)
    rest = x - hi.astype(jnp.float32)
    mid = rest.astype(jnp.bfloat16)
    lo = (rest - mid.astype(jnp.float32)).astype(jnp.bfloat16)
    return hi, mid, lo


def nt_dot(a, b):
    return lax.dot_general(a, b, (((1,), (1,)), ((), ())), preferred_element_type=jnp.float32)


def kernel(
    n,
    q_hbm,
    docs_hbm,
    lengths_hbm,
    cand_hbm,
    out_ref,
    docs,
    lengths,
    cand,
    queries,
    best,
    scores,
    table,
    doc_sem,
    small_sem,
    q_send,
    q_recv,
    s_send,
    s_recv,
):
    me = lax.axis_index("doc")
    count, doc_len, feature = docs.shape
    query_len = queries.shape[1]
    width = min(n, LANES // query_len)
    groups = n // width
    home = me // width
    place = lax.rem(me, width)
    chunk = count // CHUNKS

    own = pltpu.make_async_copy(q_hbm.at[0], queries.at[me], small_sem.at[0])
    own.start()
    len_copy = pltpu.make_async_copy(lengths_hbm, lengths, small_sem.at[1])
    len_copy.start()

    def doc_copy(c):
        rows = pl.ds(c * chunk, chunk)
        return pltpu.make_async_copy(docs_hbm.at[rows], docs.at[rows], doc_sem.at[c])

    @pl.loop(0, CHUNKS)
    def _(c):
        doc_copy(c).start()

    cand_copy = pltpu.make_async_copy(cand_hbm, cand, small_sem.at[2])
    cand_copy.start()

    barrier = pltpu.get_barrier_semaphore()

    @pl.loop(1, n)
    def _(p):
        pl.semaphore_signal(
            barrier,
            inc=1,
            device_id={"doc": lax.rem(me + p, n)},
            device_id_type=pl.DeviceIdType.MESH,
        )

    len_copy.wait()
    rows_of = lax.broadcasted_iota(jnp.int32, (doc_len, feature), 0)

    @pl.loop(0, CHUNKS)
    def _(c):
        doc_copy(c).wait()

        @pl.loop(0, chunk, unroll=4)
        def _(i):
            d = c * chunk + i
            doc = docs[d]
            docs[d] = jnp.where(rows_of < lengths[0, d], doc, doc[0:1])

    own.wait()
    pl.semaphore_wait(barrier, n - 1)

    def query_copy(peer):
        return pltpu.make_async_remote_copy(
            src_ref=queries.at[me],
            dst_ref=queries.at[me],
            send_sem=q_send.at[0],
            recv_sem=q_recv.at[home],
            device_id={"doc": peer},
            device_id_type=pl.DeviceIdType.MESH,
        )

    def score_copy(peer):
        return pltpu.make_async_remote_copy(
            src_ref=scores.at[peer],
            dst_ref=table.at[me],
            send_sem=s_send.at[0],
            recv_sem=s_recv.at[0],
            device_id={"doc": peer},
            device_id_type=pl.DeviceIdType.MESH,
        )

    def wait_slots(ref, slots, sem):
        part = ref.at[pl.ds(0, slots)]
        pltpu.make_async_copy(part, part, sem).wait()


    def peer_at(g, j):
        return lax.rem(home + g, groups) * width + lax.rem(place + j, width)

    @pl.loop(1, n)
    def _(p):
        query_copy(peer_at(p // width, lax.rem(p, width))).start()

    lane_query = lax.broadcasted_iota(jnp.int32, (width, width * query_len), 1) // query_len
    row_query = lax.broadcasted_iota(jnp.int32, (width, width * query_len), 0)
    member = (lane_query == row_query).astype(jnp.bfloat16)

    @pl.loop(0, groups)
    def _(g):
        first = lax.rem(home + g, groups) * width

        @pl.when(g == 0)
        def _():
            wait_slots(queries, width - 1, q_recv.at[home])

        @pl.when(g > 0)
        def _():
            wait_slots(queries, width, q_recv.at[first // width])

        q = queries[pl.ds(first, width)].reshape(width * query_len, feature)

        @pl.loop(0, count // UNROLL)
        def _(b):
            start = pl.multiple_of(b * UNROLL, UNROLL)
            parts = []
            for u in range(UNROLL):
                similar = nt_dot(docs[start + u], q)
                parts.append(jnp.max(similar, axis=0, keepdims=True))
            best[pl.ds(start, UNROLL), :] = jnp.concatenate(parts, axis=0)

        hi, mid, lo = split3(best[...])
        total = nt_dot(member, hi) + nt_dot(member, mid) + nt_dot(member, lo)
        for j in range(width):
            scores[first + j] = total[j : j + 1]

        @pl.loop(0, width)
        def _(j):
            peer = first + lax.rem(place + j, width)

            @pl.when(peer != me)
            def _():
                score_copy(peer).start()

    table[me] = scores[me]
    cand_copy.wait()

    wait_slots(table, n - 1, s_recv.at[0])

    ids = cand[...]
    owner = ids // count
    local = ids - owner * count
    cands = ids.shape[1]
    pick = (lax.broadcasted_iota(jnp.int32, (count, cands), 0) == local).astype(jnp.bfloat16)
    hi, mid, lo = split3(table[...].reshape(n, count))
    found = (
        jnp.dot(hi, pick, preferred_element_type=jnp.float32)
        + jnp.dot(mid, pick, preferred_element_type=jnp.float32)
        + jnp.dot(lo, pick, preferred_element_type=jnp.float32)
    )
    mine = lax.broadcasted_iota(jnp.int32, (n, cands), 0) == owner
    out_ref[...] = jnp.sum(jnp.where(mine, found, 0.0), axis=0, keepdims=True)

    wait_slots(queries, n - 1, q_send.at[0])
    wait_slots(scores, n - 1, s_send.at[0])


def body(queries, doc_tokens, doc_lengths, candidates):
    n = lax.axis_size("doc")
    _, query_len, feature = queries.shape
    count, doc_len, _ = doc_tokens.shape
    cands = candidates.shape[1]
    width = min(n, LANES // query_len)
    hbm = pl.BlockSpec(memory_space=pl.ANY)
    return pl.pallas_call(
        functools.partial(kernel, n),
        out_shape=jax.ShapeDtypeStruct((1, cands), jnp.float32),
        in_specs=[hbm] * 4,
        out_specs=pl.BlockSpec(memory_space=pltpu.VMEM),
        scratch_shapes=[
            pltpu.VMEM((count, doc_len, feature), jnp.bfloat16),
            pltpu.SMEM((1, count), jnp.int32),
            pltpu.VMEM((1, cands), jnp.int32),
            pltpu.VMEM((n, query_len, feature), jnp.bfloat16),
            pltpu.VMEM((count, width * query_len), jnp.float32),
            pltpu.VMEM((n, 1, count), jnp.float32),
            pltpu.VMEM((n, 1, count), jnp.float32),
            pltpu.SemaphoreType.DMA((CHUNKS,)),
            pltpu.SemaphoreType.DMA((3,)),
            pltpu.SemaphoreType.DMA((1,)),
            pltpu.SemaphoreType.DMA((n // width,)),
            pltpu.SemaphoreType.DMA((1,)),
            pltpu.SemaphoreType.DMA((1,)),
        ],
        compiler_params=pltpu.CompilerParams(
            collective_id=0, has_side_effects=True, vmem_limit_bytes=60 * 1024 * 1024
        ),
        cost_estimate=pl.CostEstimate(
            flops=2 * n * query_len * count * doc_len * feature,
            bytes_accessed=2 * count * doc_len * feature,
            transcendentals=0,
        ),
        name="maxsim",
    )(queries, doc_tokens, doc_lengths.reshape(1, count), candidates)


def solution(mesh):
    placed = (
        P(("groups", "doc"), None, None),
        P(("groups", "doc"), None, None),
        P(("groups", "doc")),
        P(("groups", "doc"), None),
    )
    return jax.shard_map(
        body, mesh=mesh, in_specs=placed, out_specs=P(("groups", "doc"), None), check_vma=False
    )
```

```python
import functools

import jax
import jax.numpy as jnp
from jax import lax
from jax.experimental import pallas as pl
from jax.experimental.pallas import tpu as pltpu
from jax.sharding import PartitionSpec as P

LANES = 256
CHUNKS = 8
UNROLL = 128


def split3(x):
    hi = x.astype(jnp.bfloat16)
    rest = x - hi.astype(jnp.float32)
    mid = rest.astype(jnp.bfloat16)
    lo = (rest - mid.astype(jnp.float32)).astype(jnp.bfloat16)
    return hi, mid, lo


def nt_dot(a, b):
    return lax.dot_general(a, b, (((1,), (1,)), ((), ())), preferred_element_type=jnp.float32)


def kernel(
    n,
    q_hbm,
    docs_hbm,
    lengths_hbm,
    cand_hbm,
    out_ref,
    docs,
    lengths,
    cand,
    queries,
    best,
    scores,
    table,
    doc_sem,
    small_sem,
    q_send,
    q_recv,
    s_send,
    s_recv,
):
    me = lax.axis_index("doc")
    count, doc_len, feature = docs.shape
    query_len = queries.shape[1]
    width = min(n, LANES // query_len)
    groups = n // width
    home = me // width
    place = lax.rem(me, width)
    chunk = count // CHUNKS

    barrier = pltpu.get_barrier_semaphore()

    @pl.loop(1, n)
    def _(p):
        pl.semaphore_signal(
            barrier,
            inc=1,
            device_id={"doc": lax.rem(me + p, n)},
            device_id_type=pl.DeviceIdType.MESH,
        )

    own = pltpu.make_async_copy(q_hbm.at[0], queries.at[me], small_sem.at[0])
    own.start()
    len_copy = pltpu.make_async_copy(lengths_hbm, lengths, small_sem.at[1])
    len_copy.start()

    def doc_copy(c):
        rows = pl.ds(c * chunk, chunk)
        return pltpu.make_async_copy(docs_hbm.at[rows], docs.at[rows], doc_sem.at[c])

    @pl.loop(0, CHUNKS)
    def _(c):
        doc_copy(c).start()

    cand_copy = pltpu.make_async_copy(cand_hbm, cand, small_sem.at[2])
    cand_copy.start()

    own.wait()
    pl.semaphore_wait(barrier, n - 1)

    def query_copy(peer):
        return pltpu.make_async_remote_copy(
            src_ref=queries.at[me],
            dst_ref=queries.at[me],
            send_sem=q_send.at[0],
            recv_sem=q_recv.at[home],
            device_id={"doc": peer},
            device_id_type=pl.DeviceIdType.MESH,
        )

    def score_copy(peer):
        return pltpu.make_async_remote_copy(
            src_ref=scores.at[peer],
            dst_ref=table.at[me],
            send_sem=s_send.at[0],
            recv_sem=s_recv.at[0],
            device_id={"doc": peer},
            device_id_type=pl.DeviceIdType.MESH,
        )

    def wait_slots(ref, slots, sem):
        part = ref.at[pl.ds(0, slots)]
        pltpu.make_async_copy(part, part, sem).wait()

    def peer_at(g, j):
        return lax.rem(home + g, groups) * width + lax.rem(place + j, width)

    @pl.loop(1, n)
    def _(p):
        query_copy(peer_at(p // width, lax.rem(p, width))).start()

    len_copy.wait()
    rows_of = lax.broadcasted_iota(jnp.int32, (doc_len, feature), 0)

    @pl.loop(0, CHUNKS)
    def _(c):
        doc_copy(c).wait()

        @pl.loop(0, chunk, unroll=4)
        def _(i):
            d = c * chunk + i
            doc = docs[d]
            docs[d] = jnp.where(rows_of < lengths[0, d], doc, doc[0:1])

    lane_query = lax.broadcasted_iota(jnp.int32, (width, width * query_len), 1) // query_len
    row_query = lax.broadcasted_iota(jnp.int32, (width, width * query_len), 0)
    member = (lane_query == row_query).astype(jnp.bfloat16)

    @pl.loop(0, groups)
    def _(g):
        first = lax.rem(home + g, groups) * width

        @pl.when(g == 0)
        def _():
            wait_slots(queries, width - 1, q_recv.at[home])

        @pl.when(g > 0)
        def _():
            wait_slots(queries, width, q_recv.at[first // width])

        q = queries[pl.ds(first, width)].reshape(width * query_len, feature)

        @pl.loop(0, count // UNROLL)
        def _(b):
            start = pl.multiple_of(b * UNROLL, UNROLL)
            parts = []
            for u in range(UNROLL):
                similar = nt_dot(docs[start + u], q)
                parts.append(jnp.max(similar, axis=0, keepdims=True))
            best[pl.ds(start, UNROLL), :] = jnp.concatenate(parts, axis=0)

        hi, mid, lo = split3(best[...])
        total = nt_dot(member, hi) + nt_dot(member, mid) + nt_dot(member, lo)
        for j in range(width):
            scores[first + j] = total[j : j + 1]

        @pl.loop(0, width)
        def _(j):
            peer = first + lax.rem(place + j, width)

            @pl.when(peer != me)
            def _():
                score_copy(peer).start()

    table[me] = scores[me]
    cand_copy.wait()


    ids = cand[...]
    owner = ids // count
    local = ids - owner * count
    cands = ids.shape[1]
    pick = (lax.broadcasted_iota(jnp.int32, (count, cands), 0) == local).astype(jnp.bfloat16)
    wait_slots(table, n - 1, s_recv.at[0])
    hi, mid, lo = split3(table[...].reshape(n, count))
    found = (
        jnp.dot(hi, pick, preferred_element_type=jnp.float32)
        + jnp.dot(mid, pick, preferred_element_type=jnp.float32)
        + jnp.dot(lo, pick, preferred_element_type=jnp.float32)
    )
    mine = lax.broadcasted_iota(jnp.int32, (n, cands), 0) == owner
    out_ref[...] = jnp.sum(jnp.where(mine, found, 0.0), axis=0, keepdims=True)

    wait_slots(queries, n - 1, q_send.at[0])
    wait_slots(scores, n - 1, s_send.at[0])


def body(queries, doc_tokens, doc_lengths, candidates):
    n = lax.axis_size("doc")
    _, query_len, feature = queries.shape
    count, doc_len, _ = doc_tokens.shape
    cands = candidates.shape[1]
    width = min(n, LANES // query_len)
    hbm = pl.BlockSpec(memory_space=pl.ANY)
    return pl.pallas_call(
        functools.partial(kernel, n),
        out_shape=jax.ShapeDtypeStruct((1, cands), jnp.float32),
        in_specs=[hbm] * 4,
        out_specs=pl.BlockSpec(memory_space=pltpu.VMEM),
        scratch_shapes=[
            pltpu.VMEM((count, doc_len, feature), jnp.bfloat16),
            pltpu.SMEM((1, count), jnp.int32),
            pltpu.VMEM((1, cands), jnp.int32),
            pltpu.VMEM((n, query_len, feature), jnp.bfloat16),
            pltpu.VMEM((count, width * query_len), jnp.float32),
            pltpu.VMEM((n, 1, count), jnp.float32),
            pltpu.VMEM((n, 1, count), jnp.float32),
            pltpu.SemaphoreType.DMA((CHUNKS,)),
            pltpu.SemaphoreType.DMA((3,)),
            pltpu.SemaphoreType.DMA((1,)),
            pltpu.SemaphoreType.DMA((n // width,)),
            pltpu.SemaphoreType.DMA((1,)),
            pltpu.SemaphoreType.DMA((1,)),
        ],
        compiler_params=pltpu.CompilerParams(
            collective_id=0, has_side_effects=True, vmem_limit_bytes=60 * 1024 * 1024
        ),
        cost_estimate=pl.CostEstimate(
            flops=2 * n * query_len * count * doc_len * feature,
            bytes_accessed=2 * count * doc_len * feature,
            transcendentals=0,
        ),
        name="maxsim",
    )(queries, doc_tokens, doc_lengths.reshape(1, count), candidates)


def solution(mesh):
    placed = (
        P(("groups", "doc"), None, None),
        P(("groups", "doc"), None, None),
        P(("groups", "doc")),
        P(("groups", "doc"), None),
    )
    return jax.shard_map(
        body, mesh=mesh, in_specs=placed, out_specs=P(("groups", "doc"), None), check_vma=False
    )
```

```python
import functools

import jax
import jax.numpy as jnp
from jax import lax
from jax.experimental import pallas as pl
from jax.experimental.pallas import tpu as pltpu
from jax.sharding import PartitionSpec as P

LANES = 256
CHUNKS = 8
UNROLL = 128


def split3(x):
    hi = x.astype(jnp.bfloat16)
    rest = x - hi.astype(jnp.float32)
    mid = rest.astype(jnp.bfloat16)
    lo = (rest - mid.astype(jnp.float32)).astype(jnp.bfloat16)
    return hi, mid, lo


def nt_dot(a, b):
    return lax.dot_general(a, b, (((1,), (1,)), ((), ())), preferred_element_type=jnp.float32)


def kernel(
    n,
    q_hbm,
    docs_hbm,
    lengths_hbm,
    cand_hbm,
    out_ref,
    docs,
    lengths,
    cand,
    queries,
    best,
    scores,
    table,
    doc_sem,
    small_sem,
    q_send,
    q_recv,
    s_send,
    s_recv,
):
    me = lax.axis_index("doc")
    count, doc_len, feature = docs.shape
    query_len = queries.shape[1]
    width = min(n, LANES // query_len)
    groups = n // width
    home = me // width
    place = lax.rem(me, width)
    chunk = count // CHUNKS

    barrier = pltpu.get_barrier_semaphore()

    @pl.loop(1, n)
    def _(p):
        pl.semaphore_signal(
            barrier,
            inc=1,
            device_id={"doc": lax.rem(me + p, n)},
            device_id_type=pl.DeviceIdType.MESH,
        )

    own = pltpu.make_async_copy(q_hbm.at[0], queries.at[me], small_sem.at[0])
    own.start()
    len_copy = pltpu.make_async_copy(lengths_hbm, lengths, small_sem.at[1])
    len_copy.start()

    def doc_copy(c):
        rows = pl.ds(c * chunk, chunk)
        return pltpu.make_async_copy(docs_hbm.at[rows], docs.at[rows], doc_sem.at[c])

    @pl.loop(0, CHUNKS)
    def _(c):
        doc_copy(c).start()

    cand_copy = pltpu.make_async_copy(cand_hbm, cand, small_sem.at[2])
    cand_copy.start()

    own.wait()
    pl.semaphore_wait(barrier, n - 1)

    def query_copy(peer):
        return pltpu.make_async_remote_copy(
            src_ref=queries.at[me],
            dst_ref=queries.at[me],
            send_sem=q_send.at[0],
            recv_sem=q_recv.at[home],
            device_id={"doc": peer},
            device_id_type=pl.DeviceIdType.MESH,
        )

    def score_copy(peer):
        return pltpu.make_async_remote_copy(
            src_ref=scores.at[peer],
            dst_ref=table.at[me],
            send_sem=s_send.at[0],
            recv_sem=s_recv.at[0],
            device_id={"doc": peer},
            device_id_type=pl.DeviceIdType.MESH,
        )

    def wait_slots(ref, slots, sem):
        part = ref.at[pl.ds(0, slots)]
        pltpu.make_async_copy(part, part, sem).wait()

    def peer_at(g, j):
        return lax.rem(home + g, groups) * width + lax.rem(place + j, width)

    @pl.loop(1, n)
    def _(p):
        query_copy(peer_at(p // width, lax.rem(p, width))).start()

    len_copy.wait()
    rows_of = lax.broadcasted_iota(jnp.int32, (doc_len, feature), 0)

    @pl.loop(0, CHUNKS)
    def _(c):
        doc_copy(c).wait()

        @pl.loop(0, chunk, unroll=4)
        def _(i):
            d = c * chunk + i
            doc = docs[d]
            docs[d] = jnp.where(rows_of < lengths[0, d], doc, doc[0:1])

    lane_query = lax.broadcasted_iota(jnp.int32, (width, width * query_len), 1) // query_len
    row_query = lax.broadcasted_iota(jnp.int32, (width, width * query_len), 0)
    member = (lane_query == row_query).astype(jnp.bfloat16)
    members = jnp.concatenate([member] * 3, axis=1)

    @pl.loop(0, groups)
    def _(g):
        first = lax.rem(home + g, groups) * width

        @pl.when(g == 0)
        def _():
            wait_slots(queries, width - 1, q_recv.at[home])

        @pl.when(g > 0)
        def _():
            wait_slots(queries, width, q_recv.at[first // width])

        q = queries[pl.ds(first, width)].reshape(width * query_len, feature)

        @pl.loop(0, count // UNROLL)
        def _(b):
            start = pl.multiple_of(b * UNROLL, UNROLL)
            parts = []
            for u in range(UNROLL):
                similar = nt_dot(docs[start + u], q)
                parts.append(jnp.max(similar, axis=0, keepdims=True))
            best[pl.ds(start, UNROLL), :] = jnp.concatenate(parts, axis=0)

        total = nt_dot(members, jnp.concatenate(split3(best[...]), axis=1))
        for j in range(width):
            scores[first + j] = total[j : j + 1]

        @pl.loop(0, width)
        def _(j):
            peer = first + lax.rem(place + j, width)

            @pl.when(peer != me)
            def _():
                score_copy(peer).start()

    table[me] = scores[me]
    cand_copy.wait()


    ids = cand[...]
    owner = ids // count
    local = ids - owner * count
    cands = ids.shape[1]
    pick = (lax.broadcasted_iota(jnp.int32, (count, cands), 0) == local).astype(jnp.bfloat16)
    wait_slots(table, n - 1, s_recv.at[0])
    terms = jnp.concatenate(split3(table[...].reshape(n, count)), axis=0)
    found = jnp.dot(terms, pick, preferred_element_type=jnp.float32)
    found = found[:n] + found[n : 2 * n] + found[2 * n :]
    mine = lax.broadcasted_iota(jnp.int32, (n, cands), 0) == owner
    out_ref[...] = jnp.sum(jnp.where(mine, found, 0.0), axis=0, keepdims=True)

    wait_slots(queries, n - 1, q_send.at[0])
    wait_slots(scores, n - 1, s_send.at[0])


def body(queries, doc_tokens, doc_lengths, candidates):
    n = lax.axis_size("doc")
    _, query_len, feature = queries.shape
    count, doc_len, _ = doc_tokens.shape
    cands = candidates.shape[1]
    width = min(n, LANES // query_len)
    hbm = pl.BlockSpec(memory_space=pl.ANY)
    return pl.pallas_call(
        functools.partial(kernel, n),
        out_shape=jax.ShapeDtypeStruct((1, cands), jnp.float32),
        in_specs=[hbm] * 4,
        out_specs=pl.BlockSpec(memory_space=pltpu.VMEM),
        scratch_shapes=[
            pltpu.VMEM((count, doc_len, feature), jnp.bfloat16),
            pltpu.SMEM((1, count), jnp.int32),
            pltpu.VMEM((1, cands), jnp.int32),
            pltpu.VMEM((n, query_len, feature), jnp.bfloat16),
            pltpu.VMEM((count, width * query_len), jnp.float32),
            pltpu.VMEM((n, 1, count), jnp.float32),
            pltpu.VMEM((n, 1, count), jnp.float32),
            pltpu.SemaphoreType.DMA((CHUNKS,)),
            pltpu.SemaphoreType.DMA((3,)),
            pltpu.SemaphoreType.DMA((1,)),
            pltpu.SemaphoreType.DMA((n // width,)),
            pltpu.SemaphoreType.DMA((1,)),
            pltpu.SemaphoreType.DMA((1,)),
        ],
        compiler_params=pltpu.CompilerParams(
            collective_id=0, has_side_effects=True, vmem_limit_bytes=60 * 1024 * 1024
        ),
        cost_estimate=pl.CostEstimate(
            flops=2 * n * query_len * count * doc_len * feature,
            bytes_accessed=2 * count * doc_len * feature,
            transcendentals=0,
        ),
        name="maxsim",
    )(queries, doc_tokens, doc_lengths.reshape(1, count), candidates)


def solution(mesh):
    placed = (
        P(("groups", "doc"), None, None),
        P(("groups", "doc"), None, None),
        P(("groups", "doc")),
        P(("groups", "doc"), None),
    )
    return jax.shard_map(
        body, mesh=mesh, in_specs=placed, out_specs=P(("groups", "doc"), None), check_vma=False
    )
```
